32 devices in a mesh: dp: 8 (over y, x, core), mp: 4 (over z).
Axes of the slice: x: 2, y: 2, z: 4, core: 2. Of those that a mesh axis runs over, the one named last changes fastest.
Arguments:
- hidden: bfloat16 [2, 512, 4224], P(None, 'dp'), may hold values from 0 to 6, as said below
- proj_weight: bfloat16 [4224, 4224], P(None, 'mp'), may hold values from -0.09375 to 0.09375
Outputs:
- grad_first: bfloat16 [512, 4224], P('dp', 'mp')
The draws below stay inside these ranges and needn't reach their ends.
Inputs may be any that keep to these rules, and one draw needn't show every extreme that they name: `hidden`: rectified features of 512 images in two views.
All inputs are finite; a program needn't handle non-finite values.
Results may differ from the reference program's by a relative error of at most 0.0057.
Values may be sent and summed in bfloat16 or wider, within the bound.
A program may use at most 64 MiB of HBM per device.

```python
import jax
import jax.numpy as jnp
from jax import lax

HID = 4224
PROJ = 4224
IMAGES = 512


def draw_hidden(key, part):
    keys = jax.random.split(jax.random.fold_in(key, 11), 4)
    base = jax.random.normal(keys[0], (1, IMAGES, HID), jnp.float32)
    noise = 0.5 * jax.random.normal(keys[1], (2, IMAGES, HID), jnp.float32)
    factor = jax.random.normal(keys[2], (1, IMAGES, 1), jnp.float32)
    loading = jax.random.normal(keys[3], (1, 1, HID), jnp.float32)
    pre = base + noise + 0.3 * factor * loading
    return jnp.clip(pre, 0.0, 6.0).astype(jnp.bfloat16)


def steps_of(key, extent, cuts, least, high):
    level = 1.0
    for axis_at, parts in cuts:
        heights = jax.random.uniform(jax.random.fold_in(jax.random.fold_in(key, 6), axis_at), (parts,), jnp.float32, least / len(cuts), high / len(cuts))
        level = level * jnp.repeat(jnp.exp(heights), extent[axis_at] // parts).reshape((-1,) + (1,) * (len(extent) - 1 - axis_at))
    return level


def gaussian(rng, shape, spread, bound, shards=(), kind=jnp.bfloat16):
    entries = jax.random.normal(rng, shape, jnp.float32) * spread
    if len(shards) > 0:
        entries = steps_of(rng, shape, shards, -0.22, 0.18) * entries
    return jnp.clip(entries, min=-bound, max=bound).astype(kind)


def setup_inputs(seed: int = 0) -> dict:
    arg_keys = jax.random.split(jax.random.key(seed), 3)
    hidden = draw_hidden(jax.random.fold_in(arg_keys[2], 71), 0)
    proj_weight = gaussian(arg_keys[1], (HID, PROJ), HID ** -0.5, 0.09375, ((1, 4),))
    return {"hidden": hidden, "proj_weight": proj_weight}


off_weight = 0.0051
eps = 1e-05

def reference(hidden, proj_weight):
    normed = []
    scales = []
    for view in range(2):
        feats = jnp.dot(hidden[view], proj_weight, preferred_element_type=jnp.float32)
        mean = lax.optimization_barrier(jnp.sum(feats, axis=0, keepdims=True)) / IMAGES
        centered = feats - mean
        var = lax.optimization_barrier(jnp.sum(centered * centered, axis=0, keepdims=True)) / IMAGES
        normed.append((centered / jnp.sqrt(var + eps)).astype(jnp.bfloat16))
        scales.append(1.0 / jnp.sqrt(var + eps))
    first, second = (normed[0], normed[1])
    corr = jnp.dot(first.T, second, preferred_element_type=jnp.float32) / IMAGES
    ident = jnp.arange(PROJ, dtype=jnp.int32)[:, None] == jnp.arange(PROJ, dtype=jnp.int32)[None, :]
    grad_corr = jnp.where(ident, 2.0 * (corr - 1.0), 2.0 * off_weight * corr).astype(jnp.bfloat16)
    grad_wide = grad_corr.astype(jnp.float32)
    diag_val = jnp.diagonal(grad_wide)
    scale_sum = (lax.optimization_barrier(jnp.sum(grad_wide * grad_wide, axis=1)) - diag_val * diag_val) / (2.0 * off_weight) + diag_val * (1.0 + diag_val / 2.0)
    back = jnp.dot(second, grad_corr.T, preferred_element_type=jnp.float32)
    result = (back - first.astype(jnp.float32) * scale_sum[None, :]) * scales[0]
    return result.astype(jnp.bfloat16)
```

```python
import functools

import jax
import jax.numpy as jnp
from jax import lax
from jax.experimental import pallas as pl
from jax.experimental.pallas import tpu as pltpu
from jax.sharding import PartitionSpec as P

off_weight = 0.0051
eps = 1e-05
CW = 384
MESH = pl.DeviceIdType.MESH
F32 = jnp.float32
BF16 = jnp.bfloat16


def kernel(
    D, Z, n_chunk, cols, h_ref, w_ref, o_ref,
    own, blk, nrm, stats, mom, kpart, ksend, krecv, msum, qsend, qrecv,
    s_send, s_recv, s_fwd, s_frecv, t_send, t_recv, t_fwd, t_frecv,
    k_send, k_recv, q_send, q_recv,
):
    C = D // 2
    R = h_ref.shape[1]
    B = R * D
    step = pl.program_id(0)
    dp = lax.axis_index("dp")
    mp = lax.axis_index("mp")
    chip = dp // 2
    core = lax.rem(dp, 2)
    sib = chip * 2 + (1 - core)

    def peer_chip(k):
        return lax.rem(chip + k, C)

    def dev(c, k):
        return c * 2 + k

    def block_copy(v, j, k):
        return pltpu.make_async_remote_copy(
            src_ref=blk.at[v, j, dp], dst_ref=blk.at[v, j, dp],
            send_sem=s_send.at[v, j, k], recv_sem=s_recv.at[v, j, C - k],
            device_id=(dev(peer_chip(k), core), mp), device_id_type=MESH)

    def block_fwd(v, j, k):
        src = dev(peer_chip(k), core)
        return pltpu.make_async_remote_copy(
            src_ref=blk.at[v, j, src], dst_ref=blk.at[v, j, src],
            send_sem=s_fwd.at[v, j, k], recv_sem=s_frecv.at[v, j, k],
            device_id=(sib, mp), device_id_type=MESH)

    def block_in(v, j, k):
        src = dev(peer_chip(k), core)
        return pltpu.make_async_remote_copy(
            src_ref=blk.at[v, j, src], dst_ref=blk.at[v, j, src],
            send_sem=s_send.at[v, j, k], recv_sem=s_recv.at[v, j, k],
            device_id=(sib, mp), device_id_type=MESH)

    def block_fin(v, j, k):
        src = dev(peer_chip(k), 1 - core)
        return pltpu.make_async_remote_copy(
            src_ref=blk.at[v, j, src], dst_ref=blk.at[v, j, src],
            send_sem=s_fwd.at[v, j, k], recv_sem=s_frecv.at[v, j, k],
            device_id=(sib, mp), device_id_type=MESH)

    def stat_copy(k):
        return pltpu.make_async_remote_copy(
            src_ref=stats.at[dp], dst_ref=stats.at[dp],
            send_sem=t_send.at[k], recv_sem=t_recv.at[D - k],
            device_id=(lax.rem(dp + k, D), mp), device_id_type=MESH)

    def stat_in(k):
        src = lax.rem(dp + k, D)
        return pltpu.make_async_remote_copy(
            src_ref=stats.at[src], dst_ref=stats.at[src],
            send_sem=t_send.at[k], recv_sem=t_recv.at[k],
            device_id=(src, mp), device_id_type=MESH)

    def k_copy(k):
        return pltpu.make_async_remote_copy(
            src_ref=ksend, dst_ref=krecv.at[Z - k],
            send_sem=k_send.at[k], recv_sem=k_recv.at[Z - k],
            device_id=(dp, lax.rem(mp + k, Z)), device_id_type=MESH)

    def k_in(k):
        return pltpu.make_async_remote_copy(
            src_ref=ksend, dst_ref=krecv.at[k],
            send_sem=k_send.at[k], recv_sem=k_recv.at[k],
            device_id=(dp, lax.rem(mp + k, Z)), device_id_type=MESH)

    def q_copy(k):
        return pltpu.make_async_remote_copy(
            src_ref=qsend, dst_ref=qrecv.at[D - k],
            send_sem=q_send.at[k], recv_sem=q_recv.at[D - k],
            device_id=(lax.rem(dp + k, D), mp), device_id_type=MESH)

    def q_in(k):
        return pltpu.make_async_remote_copy(
            src_ref=qsend, dst_ref=qrecv.at[k],
            send_sem=q_send.at[k], recv_sem=q_recv.at[k],
            device_id=(lax.rem(dp + k, D), mp), device_id_type=MESH)

    def each(lo, hi, f):
        def body(k, _):
            f(k)
            return 0
        lax.fori_loop(lo, hi, body, 0)

    barrier = pltpu.get_barrier_semaphore()

    @pl.when(step == 0)
    def _():
        each(1, D, lambda k: pl.semaphore_signal(
            barrier, inc=1, device_id=(lax.rem(dp + k, D), mp), device_id_type=MESH))
        each(1, Z, lambda k: pl.semaphore_signal(
            barrier, inc=1, device_id=(dp, lax.rem(mp + k, Z)), device_id_type=MESH))

    f = jnp.dot(h_ref[...].reshape(2 * R, h_ref.shape[2]), w_ref[...], preferred_element_type=F32)
    lane = step * CW + lax.broadcasted_iota(jnp.int32, (1, CW), 1)
    f = jnp.where(lane < cols, f, 0.0)
    for v in range(2):
        fv = f[v * R:(v + 1) * R]
        mean = jnp.sum(fv, axis=0, keepdims=True) / R
        c = fv - mean
        m2 = jnp.sum(c * c, axis=0, keepdims=True)
        own[v, step] = c
        blk[v, step, dp] = c.astype(BF16)
        stats[dp, 2 * v, step] = mean[0]
        stats[dp, 2 * v + 1, step] = m2[0]

    @pl.when(step == 0)
    def _():
        pl.semaphore_wait(barrier, D - 1 + Z - 1)

    def send(v, j):
        each(1, C, lambda k: block_copy(v, j, k).start())
        block_fwd(v, j, 0).start()

    send(1, step)

    @pl.when(step == n_chunk - 1)
    def _():
        each(1, D, lambda k: stat_copy(k).start())
        for j in range(n_chunk):
            send(0, j)

        def forward(v):
            for j in range(n_chunk):
                def go(k, j=j):
                    block_in(v, j, k).wait_recv()
                    block_fwd(v, j, k).start()
                each(1, C, go)

        def moments(v, j):
            mean = jnp.mean(stats[:, 2 * v, j], axis=0, keepdims=True)
            dev_mean = stats[:, 2 * v, j] - mean
            var = (jnp.sum(stats[:, 2 * v + 1, j], axis=0, keepdims=True)
                   + R * jnp.sum(dev_mean * dev_mean, axis=0, keepdims=True)) / B
            return mean, var

        def normalize(v):
            for j in range(n_chunk):
                each(0, C, lambda k, j=j: block_fin(v, j, k).wait_recv())
            for j in range(n_chunk):
                mean, var = moments(v, j)
                inv = 1.0 / jnp.sqrt(var + eps)
                mom[v, j, 0] = mean[0]
                mom[v, j, 1] = inv[0]

                def go(d, j=j, mean=mean, inv=inv, v=v):
                    shift = stats[d, pl.ds(2 * v, 1), j] - mean
                    nrm[v, j, d] = ((blk[v, j, d].astype(F32) + shift) * inv).astype(BF16)
                each(0, D, go)

        forward(1)
        each(1, D, lambda k: stat_in(k).wait_recv())
        normalize(1)

        G = 4
        def kgroup(g):
            acc = jnp.zeros((R, G * R), F32)
            for j in range(n_chunk):
                mine = nrm[1, j, dp]
                rest = nrm[1, j, pl.ds(g * G, G)].reshape(G * R, CW)
                acc += lax.dot_general(mine, rest, (((1,), (1,)), ((), ())),
                                       preferred_element_type=F32)
            at = pl.ds(pl.multiple_of(g * (G * R), G * R), G * R)
            kpart[:, at] = acc
            ksend[:, at] = acc.astype(BF16)
        each(0, D // G, kgroup)
        each(1, Z, lambda k: k_copy(k).start())

        forward(0)
        normalize(0)

        for j in range(n_chunk):
            def dsum(d, t, j=j):
                return t + nrm[0, j, d].astype(F32) * nrm[1, j, d].astype(F32)
            t = lax.fori_loop(0, D, dsum, jnp.zeros((R, CW), F32))
            mom[0, j, 2] = jnp.sum(t, axis=0) / B

        each(1, Z, lambda k: k_in(k).wait_recv())
        kb = lax.fori_loop(1, Z, lambda k, t: t + krecv[k].astype(F32), kpart[...]).astype(BF16)
        for j in range(n_chunk):
            m = jnp.dot(kb, nrm[0, j].reshape(B, CW), preferred_element_type=F32)
            msum[j] = m
            qsend[0, j] = jnp.sum(m * nrm[0, j, dp].astype(F32), axis=0)
        each(1, D, lambda k: q_copy(k).start())

        def own_norm(v, j):
            mean = mom[v, j, pl.ds(0, 1)]
            inv = mom[v, j, pl.ds(1, 1)]
            shift = stats[dp, pl.ds(2 * v, 1), j] - mean
            return ((own[v, j] + shift) * inv).astype(BF16).astype(F32)

        each(1, D, lambda k: q_in(k).wait_recv())
        for j in range(n_chunk):
            w = min(CW, cols - j * CW)
            q = lax.fori_loop(1, D, lambda k, t, j=j: t + qrecv[k, :, j],
                              qsend[:, j]) / (float(B) * B)
            cd = mom[0, j, pl.ds(2, 1)]
            inv = mom[0, j, pl.ds(1, 1)]
            g = (2.0 * (cd - 1.0)).astype(BF16).astype(F32)
            scale = 2.0 * off_weight * (q - cd * cd) + g * (1.0 + g / 2.0)
            res = ((2.0 * off_weight / B) * msum[j]
                   + own_norm(1, j) * (g - 2.0 * off_weight * cd)
                   - own_norm(0, j) * scale) * inv
            o_ref[:, j * CW:j * CW + w] = res[:, :w].astype(BF16)

        for v in range(2):
            for j in range(n_chunk):
                each(1, C, lambda k, v=v, j=j: block_copy(v, j, k).wait_send())
                each(0, C, lambda k, v=v, j=j: block_fwd(v, j, k).wait_send())
        each(1, D, lambda k: stat_copy(k).wait_send())
        each(1, Z, lambda k: k_copy(k).wait_send())
        each(1, D, lambda k: q_copy(k).wait_send())


def shards(D, Z, hidden, w):
    _, R, H = hidden.shape
    cols = w.shape[1]
    n = pl.cdiv(cols, CW)
    B = R * D
    dma = pltpu.SemaphoreType.DMA
    C = D // 2
    return pl.pallas_call(
        functools.partial(kernel, D, Z, n, cols),
        grid=(n,),
        out_shape=jax.ShapeDtypeStruct((R, cols), BF16),
        in_specs=[
            pl.BlockSpec((2, R, H), lambda i: (0, 0, 0)),
            pl.BlockSpec((H, CW), lambda i: (0, i)),
        ],
        out_specs=pl.BlockSpec((R, cols), lambda i: (0, 0)),
        scratch_shapes=[
            pltpu.VMEM((2, n, R, CW), F32),
            pltpu.VMEM((2, n, D, R, CW), BF16),
            pltpu.VMEM((2, n, D, R, CW), BF16),
            pltpu.VMEM((D, 4, n, CW), F32),
            pltpu.VMEM((2, n, 4, CW), F32),
            pltpu.VMEM((R, B), F32),
            pltpu.VMEM((R, B), BF16),
            pltpu.VMEM((Z, R, B), BF16),
            pltpu.VMEM((n, R, CW), F32),
            pltpu.VMEM((1, n, CW), F32),
            pltpu.VMEM((D, 1, n, CW), F32),
            dma((2, n, C)), dma((2, n, C)), dma((2, n, C)), dma((2, n, C)),
            dma((D,)), dma((D,)), dma((D,)), dma((D,)),
            dma((Z,)), dma((Z,)),
            dma((D,)), dma((D,)),
        ],
        compiler_params=pltpu.CompilerParams(
            collective_id=0, has_side_effects=True, vmem_limit_bytes=56 * 2**20,
            dimension_semantics=("arbitrary",)),
        cost_estimate=pl.CostEstimate(
            flops=4 * R * H * cols, bytes_accessed=2 * H * cols, transcendentals=0),
    )(hidden, w)


def solution(mesh):
    D, Z = mesh.shape["dp"], mesh.shape["mp"]
    return jax.shard_map(
        functools.partial(shards, D, Z),
        mesh=mesh,
        in_specs=(P(None, "dp", None), P(None, "mp")),
        out_specs=P("dp", "mp"),
        check_vma=False,
    )
```

```python
import functools

import jax
import jax.numpy as jnp
from jax import lax
from jax.experimental import pallas as pl
from jax.experimental.pallas import tpu as pltpu
from jax.sharding import PartitionSpec as P

off_weight = 0.0051
eps = 1e-05
CW = 384
MESH = pl.DeviceIdType.MESH
F32 = jnp.float32
BF16 = jnp.bfloat16


def kernel(
    D, Z, n_chunk, cols, h_hbm, w_hbm, o_ref,
    h_ref, w_ref, own, blk, nrm, stats, mom, kpart, ksend, krecv, msum, qsend, qrecv,
    s_send, s_recv, s_fwd, s_frecv, t_send, t_recv, t_fwd, t_frecv,
    k_send, k_recv, q_send, q_recv, h_sem, w_sem,
):
    C = D // 2
    R = h_hbm.shape[1]
    B = R * D
    dp = lax.axis_index("dp")
    mp = lax.axis_index("mp")
    chip = dp // 2
    core = lax.rem(dp, 2)
    sib = chip * 2 + (1 - core)

    def peer_chip(k):
        return lax.rem(chip + k, C)

    def dev(c, k):
        return c * 2 + k

    def block_copy(v, j, k):
        return pltpu.make_async_remote_copy(
            src_ref=blk.at[v, dp, j], dst_ref=blk.at[v, dp, j],
            send_sem=s_send.at[v, j, k], recv_sem=s_recv.at[v, j, C - k],
            device_id=(dev(peer_chip(k), core), mp), device_id_type=MESH)

    def block_fwd(v, j, k):
        src = dev(peer_chip(k), core)
        return pltpu.make_async_remote_copy(
            src_ref=blk.at[v, src, j], dst_ref=blk.at[v, src, j],
            send_sem=s_fwd.at[v, j, k], recv_sem=s_frecv.at[v, j, k],
            device_id=(sib, mp), device_id_type=MESH)

    def block_in(v, j, k):
        src = dev(peer_chip(k), core)
        return pltpu.make_async_remote_copy(
            src_ref=blk.at[v, src, j], dst_ref=blk.at[v, src, j],
            send_sem=s_send.at[v, j, k], recv_sem=s_recv.at[v, j, k],
            device_id=(sib, mp), device_id_type=MESH)

    def block_fin(v, j, k):
        src = dev(peer_chip(k), 1 - core)
        return pltpu.make_async_remote_copy(
            src_ref=blk.at[v, src, j], dst_ref=blk.at[v, src, j],
            send_sem=s_fwd.at[v, j, k], recv_sem=s_frecv.at[v, j, k],
            device_id=(sib, mp), device_id_type=MESH)

    def stat_copy(k):
        return pltpu.make_async_remote_copy(
            src_ref=stats.at[dp], dst_ref=stats.at[dp],
            send_sem=t_send.at[k], recv_sem=t_recv.at[D - k],
            device_id=(lax.rem(dp + k, D), mp), device_id_type=MESH)

    def stat_in(k):
        src = lax.rem(dp + k, D)
        return pltpu.make_async_remote_copy(
            src_ref=stats.at[src], dst_ref=stats.at[src],
            send_sem=t_send.at[k], recv_sem=t_recv.at[k],
            device_id=(src, mp), device_id_type=MESH)

    def k_copy(k):
        return pltpu.make_async_remote_copy(
            src_ref=ksend, dst_ref=krecv.at[Z - k],
            send_sem=k_send.at[k], recv_sem=k_recv.at[Z - k],
            device_id=(dp, lax.rem(mp + k, Z)), device_id_type=MESH)

    def k_in(k):
        return pltpu.make_async_remote_copy(
            src_ref=ksend, dst_ref=krecv.at[k],
            send_sem=k_send.at[k], recv_sem=k_recv.at[k],
            device_id=(dp, lax.rem(mp + k, Z)), device_id_type=MESH)

    def q_copy(k):
        return pltpu.make_async_remote_copy(
            src_ref=qsend, dst_ref=qrecv.at[D - k],
            send_sem=q_send.at[k], recv_sem=q_recv.at[D - k],
            device_id=(lax.rem(dp + k, D), mp), device_id_type=MESH)

    def q_in(k):
        return pltpu.make_async_remote_copy(
            src_ref=qsend, dst_ref=qrecv.at[k],
            send_sem=q_send.at[k], recv_sem=q_recv.at[k],
            device_id=(lax.rem(dp + k, D), mp), device_id_type=MESH)

    def each(lo, hi, f):
        def body(k, _):
            f(k)
            return 0
        lax.fori_loop(lo, hi, body, 0)

    barrier = pltpu.get_barrier_semaphore()

    each(1, D, lambda k: pl.semaphore_signal(
        barrier, inc=1, device_id=(lax.rem(dp + k, D), mp), device_id_type=MESH))
    each(1, Z, lambda k: pl.semaphore_signal(
        barrier, inc=1, device_id=(dp, lax.rem(mp + k, Z)), device_id_type=MESH))

    h_load = pltpu.make_async_copy(h_hbm, h_ref, h_sem)
    h_load.start()
    w_loads = []
    for j in range(n_chunk):
        at = pl.ds(j * CW, min(CW, cols - j * CW))
        w_loads.append(pltpu.make_async_copy(w_hbm.at[at], w_ref.at[at], w_sem.at[j]))
        w_loads[j].start()
    h_load.wait()

    def send(v, j):
        each(1, C, lambda k: block_copy(v, j, k).start())
        block_fwd(v, j, 0).start()

    for j in range(n_chunk):
        w_loads[j].wait()
        f = lax.dot_general(h_ref[...].reshape(2 * R, h_ref.shape[2]), w_ref[pl.ds(j * CW, CW)],
                            (((1,), (1,)), ((), ())), preferred_element_type=F32)
        lane = j * CW + lax.broadcasted_iota(jnp.int32, (1, CW), 1)
        f = jnp.where(lane < cols, f, 0.0)
        for v in range(2):
            fv = f[v * R:(v + 1) * R]
            mean = jnp.sum(fv, axis=0, keepdims=True) / R
            c = fv - mean
            m2 = jnp.sum(c * c, axis=0, keepdims=True)
            own[v, j] = c
            blk[v, dp, j] = c.astype(BF16)
            stats[dp, 2 * v, j] = mean[0]
            stats[dp, 2 * v + 1, j] = m2[0]
        if j == 0:
            pl.semaphore_wait(barrier, D - 1 + Z - 1)
        send(1, j)

    each(1, D, lambda k: stat_copy(k).start())
    for j in range(n_chunk):
        send(0, j)

    def forward(v):
        for j in range(n_chunk):
            def go(k, j=j):
                block_in(v, j, k).wait_recv()
                block_fwd(v, j, k).start()
            each(1, C, go)

    def moments(v, j):
        mean = jnp.mean(stats[:, 2 * v, j], axis=0, keepdims=True)
        dev_mean = stats[:, 2 * v, j] - mean
        var = (jnp.sum(stats[:, 2 * v + 1, j], axis=0, keepdims=True)
               + R * jnp.sum(dev_mean * dev_mean, axis=0, keepdims=True)) / B
        return mean, var

    def normalize(v):
        scales = []
        for j in range(n_chunk):
            mean, var = moments(v, j)
            inv = 1.0 / jnp.sqrt(var + eps)
            mom[v, j, 0] = mean[0]
            mom[v, j, 1] = inv[0]
            scales.append((mean, inv))

        def one(d):
            for j in range(n_chunk):
                mean, inv = scales[j]
                shift = stats[d, pl.ds(2 * v, 1), j] - mean
                nrm[v, j, d] = ((blk[v, d, j].astype(F32) + shift) * inv).astype(BF16)

        each(0, C, lambda k: one(dev(peer_chip(k), core)))
        def late(k):
            for j in range(n_chunk):
                block_fin(v, j, k).wait_recv()
            one(dev(peer_chip(k), 1 - core))
        each(0, C, late)

    forward(1)
    each(1, D, lambda k: stat_in(k).wait_recv())
    normalize(1)

    G = 4
    def kgroup(g):
        acc = jnp.zeros((R, G * R), F32)
        for j in range(n_chunk):
            mine = nrm[1, j, dp]
            rest = nrm[1, j, pl.ds(g * G, G)].reshape(G * R, CW)
            acc += lax.dot_general(mine, rest, (((1,), (1,)), ((), ())),
                                   preferred_element_type=F32)
        at = pl.ds(pl.multiple_of(g * (G * R), G * R), G * R)
        kpart[:, at] = acc
        ksend[:, at] = acc.astype(BF16)
    each(0, D // G, kgroup)
    each(1, Z, lambda k: k_copy(k).start())

    forward(0)
    normalize(0)

    for j in range(n_chunk):
        def dsum(d, t, j=j):
            return t + nrm[0, j, d].astype(F32) * nrm[1, j, d].astype(F32)
        t = lax.fori_loop(0, D, dsum, jnp.zeros((R, CW), F32))
        mom[0, j, 2] = jnp.sum(t, axis=0) / B

    each(1, Z, lambda k: k_in(k).wait_recv())
    kb = lax.fori_loop(1, Z, lambda k, t: t + krecv[k].astype(F32), kpart[...]).astype(BF16)
    for j in range(n_chunk):
        m = jnp.dot(kb, nrm[0, j].reshape(B, CW), preferred_element_type=F32)
        msum[j] = m
        qsend[0, j] = jnp.sum(m * nrm[0, j, dp].astype(F32), axis=0)
    each(1, D, lambda k: q_copy(k).start())

    def own_norm(v, j):
        mean = mom[v, j, pl.ds(0, 1)]
        inv = mom[v, j, pl.ds(1, 1)]
        shift = stats[dp, pl.ds(2 * v, 1), j] - mean
        return ((own[v, j] + shift) * inv).astype(BF16).astype(F32)

    each(1, D, lambda k: q_in(k).wait_recv())
    for j in range(n_chunk):
        w = min(CW, cols - j * CW)
        q = lax.fori_loop(1, D, lambda k, t, j=j: t + qrecv[k, :, j],
                          qsend[:, j]) / (float(B) * B)
        cd = mom[0, j, pl.ds(2, 1)]
        inv = mom[0, j, pl.ds(1, 1)]
        g = (2.0 * (cd - 1.0)).astype(BF16).astype(F32)
        scale = 2.0 * off_weight * (q - cd * cd) + g * (1.0 + g / 2.0)
        res = ((2.0 * off_weight / B) * msum[j]
               + own_norm(1, j) * (g - 2.0 * off_weight * cd)
               - own_norm(0, j) * scale) * inv
        o_ref[:, j * CW:j * CW + w] = res[:, :w].astype(BF16)

    for v in range(2):
        for j in range(n_chunk):
            each(1, C, lambda k: block_copy(v, j, k).wait_send())
            each(0, C, lambda k: block_fwd(v, j, k).wait_send())
    each(1, D, lambda k: stat_copy(k).wait_send())
    each(1, Z, lambda k: k_copy(k).wait_send())
    each(1, D, lambda k: q_copy(k).wait_send())


def shards(D, Z, hidden, w):
    _, R, H = hidden.shape
    cols = w.shape[1]
    n = pl.cdiv(cols, CW)
    B = R * D
    dma = pltpu.SemaphoreType.DMA
    C = D // 2
    return pl.pallas_call(
        functools.partial(kernel, D, Z, n, cols),
        out_shape=jax.ShapeDtypeStruct((R, cols), BF16),
        in_specs=[
            pl.BlockSpec(memory_space=pl.ANY),
            pl.BlockSpec(memory_space=pl.ANY),
        ],
        out_specs=pl.BlockSpec(memory_space=pltpu.VMEM),
        scratch_shapes=[
            pltpu.VMEM((2, R, H), BF16),
            pltpu.VMEM((n * CW, H), BF16),
            pltpu.VMEM((2, n, R, CW), F32),
            pltpu.VMEM((2, D, n, R, CW), BF16),
            pltpu.VMEM((2, n, D, R, CW), BF16),
            pltpu.VMEM((D, 4, n, CW), F32),
            pltpu.VMEM((2, n, 4, CW), F32),
            pltpu.VMEM((R, B), F32),
            pltpu.VMEM((R, B), BF16),
            pltpu.VMEM((Z, R, B), BF16),
            pltpu.VMEM((n, R, CW), F32),
            pltpu.VMEM((1, n, CW), F32),
            pltpu.VMEM((D, 1, n, CW), F32),
            dma((2, n, C)), dma((2, n, C)), dma((2, n, C)), dma((2, n, C)),
            dma((D,)), dma((D,)), dma((D,)), dma((D,)),
            dma((Z,)), dma((Z,)),
            dma((D,)), dma((D,)),
            dma, dma((n,)),
        ],
        compiler_params=pltpu.CompilerParams(
            collective_id=0, has_side_effects=True, vmem_limit_bytes=56 * 2**20),
        cost_estimate=pl.CostEstimate(
            flops=4 * R * H * cols, bytes_accessed=2 * H * cols, transcendentals=0),
    )(hidden, w.T)


def solution(mesh):
    D, Z = mesh.shape["dp"], mesh.shape["mp"]
    return jax.shard_map(
        functools.partial(shards, D, Z),
        mesh=mesh,
        in_specs=(P(None, "dp", None), P(None, "mp")),
        out_specs=P("dp", "mp"),
        check_vma=False,
    )
```
